256 devices in a mesh: ctx: 64 (over y_hi, x, z), head: 4 (over y_lo, core).
Axes of the slice: x: 4, y: 4 (y_hi: 2, y_lo: 2; y = y_hi * 2 + y_lo), z: 8, core: 2. Of those that a mesh axis runs over, the one named last changes fastest.
Arguments:
- queries: bfloat16 [32768, 8192], P('ctx', 'head'), may hold values from -80 to 80
- keys: bfloat16 [32768, 1024], P(('ctx', 'head')), may hold values from -4 to 4
- values: bfloat16 [32768, 1024], P(('ctx', 'head')), may hold values from -6 to 6
- lengths: int32 [64], replicated, may hold values from 1 to 1024, 32768 in all
Outputs:
- attended: bfloat16 [32768, 8192], P('ctx', 'head')
The draws below stay inside these ranges and needn't reach their ends.
Inputs may be any that keep to these rules, and one draw needn't show every extreme that they name: lengths sum to 32768; each document has 1 to 1024 tokens and one has exactly 1024.
All inputs are finite; a program needn't handle non-finite values.
Results may differ from the reference program's by a relative error of at most 0.0036.
Values may be sent and summed in bfloat16 or wider, within the bound.
A program may use at most 64 MiB of HBM per device.

```python
import math
import jax
import jax.numpy as jnp
import numpy as np
from jax import lax

HEADS = 64
KV_HEADS = 8
HD = 128
TOK_DEV = 512
REACH = 2
TOKENS = 32768
DOC_MOST = 1024
NDOC = 64
N_CTX = 64


def base_keys(key):
    return jnp.clip(jax.random.normal(key, (TOKENS, KV_HEADS * HD), jnp.float32), -4.0, 4.0)


def draw_keys(key, part):
    table = base_keys(key)
    return table.astype(jnp.bfloat16)


def draw_queries(key, part):
    key = jax.random.fold_in(key, 5)
    result = jnp.clip(jax.random.normal(key, (TOKENS, HEADS * HD), jnp.float32), -4.0, 4.0)
    return result.astype(jnp.bfloat16)


def shard_levels(rng, dims, pieces, low, high):
    loudness = 1.0
    for dim, shards_of in pieces:
        steps = jax.random.uniform(jax.random.fold_in(jax.random.fold_in(rng, 6), dim), (shards_of,), jnp.float32, low / len(pieces), high / len(pieces))
        loudness = loudness * jnp.repeat(jnp.exp(steps), dims[dim] // shards_of).reshape((-1,) + (1,) * (len(dims) - 1 - dim))
    return loudness


def length_profile(count, total, most, slope):
    weights = [(1 << 20) // math.isqrt(rank ** slope) + 1 for rank in range(2, count + 1)]
    surplus, counts = total - most - (count - 1), [1] * (count - 1)
    while surplus > 0:
        candidates = [i for i in range(count - 1) if counts[i] < most]
        pool, left = sum([weights[i] for i in candidates]), surplus
        for i in candidates:
            more = min(most - counts[i], max(1, left * weights[i] // pool), surplus)
            counts[i] = counts[i] + more
            surplus = surplus - more
    return np.array([most] + counts)


def ragged(rng, amount, total, reach, skew):
    if amount == 2:
        one = jax.random.randint(rng, (), max(1, total - reach), min(reach, total - 1) + 1)
        return jnp.stack([one, total - one])
    sizes = jnp.asarray(length_profile(amount, total, reach, skew), jnp.int32)
    twos = (amount - 1) // 2
    giver, receiver = sizes[1:1 + 2 * twos:2], sizes[2:2 + 2 * twos:2]
    slack = jnp.minimum(giver - 1, reach - receiver)
    shifted = jax.random.randint(jax.random.fold_in(rng, 1), (twos,), 0, 1 << 20) % (slack + 1)
    sizes = sizes.at[1:1 + 2 * twos:2].set(giver - shifted).at[2:2 + 2 * twos:2].set(receiver + shifted)
    return sizes[jax.random.permutation(jax.random.fold_in(rng, 2), amount)]


def scatter_about(key, dims, scale, bound, shards=(), kind=jnp.bfloat16):
    level = shard_levels(key, dims, shards, -0.22, 0.18) if shards else 1.0
    array = jax.random.normal(key, dims, jnp.float32) * scale * level
    return jnp.minimum(jnp.maximum(array, -bound), bound).astype(kind)


def setup_inputs(seed: int = 0) -> dict:
    seeds = jax.random.split(jax.random.key(seed), 5)
    return {
        "queries": draw_queries(jax.random.fold_in(seeds[4], 71), 0),
        "keys": draw_keys(jax.random.fold_in(seeds[4], 71), 0),
        "values": scatter_about(seeds[2], (TOKENS, KV_HEADS * HD), 1.0, 6.0, ((0, 256),)),
        "lengths": ragged(seeds[3], NDOC, TOKENS, DOC_MOST, 2).astype(jnp.int32),
    }


def document_of(positions, doc_ends):
    counted = jnp.sum((positions[:, None] >= doc_ends[None, :]).astype(jnp.int32), axis=1)
    return jnp.where(positions < 0, -1, counted).astype(jnp.int32)


def reference(queries, keys, values, lengths):
    group = HEADS // KV_HEADS
    key_width = (REACH + 1) * TOK_DEV
    doc_ends = jnp.cumsum(lengths).astype(jnp.int32)
    margin = jnp.zeros((REACH * TOK_DEV, KV_HEADS * HD), keys.dtype)
    padded_keys = jnp.concatenate([margin, keys], axis=0)
    padded_values = jnp.concatenate([margin, values], axis=0)
    scale = HD ** -0.5

    def one_block(block):
        start = (block * TOK_DEV).astype(jnp.int32)
        query_pos = start + jnp.arange(TOK_DEV, dtype=jnp.int32)
        key_pos = start - REACH * TOK_DEV + jnp.arange(key_width, dtype=jnp.int32)
        allowed = (document_of(query_pos, doc_ends)[:, None] == document_of(key_pos, doc_ends)[None, :]) & (key_pos[None, :] <= query_pos[:, None])
        qblock = lax.dynamic_slice_in_dim(queries, start, TOK_DEV, 0).astype(jnp.float32).reshape(TOK_DEV, KV_HEADS, group, HD)
        kblock = lax.dynamic_slice_in_dim(padded_keys, start, key_width, 0).astype(jnp.float32).reshape(key_width, KV_HEADS, HD)
        vblock = lax.dynamic_slice_in_dim(padded_values, start, key_width, 0).astype(jnp.float32).reshape(key_width, KV_HEADS, HD)
        scores = jnp.einsum('qkgd,wkd->kgqw', qblock, kblock) * scale
        scores = jnp.where(allowed[None, None], scores, -jnp.inf)
        top = jnp.max(scores, axis=-1, keepdims=True)
        weights = jnp.where(allowed[None, None], jnp.exp(scores - top), 0.0)
        total = jnp.sum(weights, axis=-1)
        rounded = lax.optimization_barrier(weights.astype(jnp.bfloat16)).astype(jnp.float32)
        mixed = jnp.einsum('kgqw,wkd->qkgd', rounded, vblock) / jnp.transpose(total, (2, 0, 1))[..., None]
        return mixed.reshape(TOK_DEV, HEADS * HD).astype(jnp.bfloat16)

    blocks = lax.map(one_block, jnp.arange(N_CTX, dtype=jnp.int32))
    return blocks.reshape(TOKENS, HEADS * HD)
```

```python
import functools

import jax
import jax.numpy as jnp
from jax import lax
from jax.experimental import pallas as pl
from jax.experimental.pallas import tpu as pltpu
from jax.sharding import PartitionSpec as P

HD = 128
SCALE = 128**-0.5 * 1.4426950408889634
NEG = -1e30
BF16 = jnp.bfloat16
F32 = jnp.float32
MESH = pl.DeviceIdType.MESH
UNROLL = 4


def dot(a, b, ca, cb):
    return lax.dot_general(a, b, (((ca,), (cb,)), ((), ())), preferred_element_type=F32)


def kernel(
    n, q_hbm, k_hbm, v_hbm, len_hbm, out, qv, ko, vo, k1a, v1a, k1b, v1b, k2h, v2h, k2l, v2l, krel, vrel,
    bo, b1a, b1b, b2h, b2l, acc, top, sb, lens, loc, a_send, a_recv, s1, r1, s2, r2, sr, rr, sf,
):
    c = lax.axis_index("ctx")
    h = lax.axis_index("head")
    hx = [h, (h // 2) * 2 + 1 - h % 2, (1 - h // 2) * 2 + h % 2, 3 - h]
    hh = h // 2
    z = c % 8
    inner = c < n - 8
    has_next = c < n - 1
    has_prev = c > 0
    to_relay = (z == 6) & inner
    relays = (z == 3) & inner
    passes = has_prev & has_next & (z != 7)

    def cols(g):
        return pl.ds(pl.multiple_of(g * 256, 256), 256)

    def rows(b):
        return pl.ds(pl.multiple_of(b * 128, 128), 128)

    src, own, rel = (k_hbm, v_hbm), (ko, vo), (krel, vrel)
    one = ((k1a, v1a), (k1a, v1a), (k1b, v1b), (k1b, v1b))
    two = (((k2l, v2l), (k2h, v2h)), ((k2h, v2h), (k2l, v2l)))

    def remote(a, b, send, recv, device):
        return pltpu.make_async_remote_copy(
            a, b, send, recv, device_id=device, device_id_type=MESH
        )

    def exchange(d):
        return [
            remote(src[t].at[:, cols(hx[d])], own[t].at[rows(h)], a_send.at[d, t], a_recv.at[d, t], (c, hx[d]))
            for t in (0, 1)
        ]

    def piece(d, t):
        return src[t].at[:, cols(h)] if d == 0 else own[t].at[rows(hx[d])]

    def first(d):
        return [
            remote(piece(d, t), one[d][t].at[rows(hx[d] % 2)], s1.at[d, t], r1.at[d, t], (c + 1, h))
            for t in (0, 1)
        ]

    def second(d, half):
        return [
            remote(
                one[d][t].at[rows(hx[d] % 2)], two[half][d // 2][t].at[rows(hx[d] % 2)],
                s2.at[d, t], r2.at[d, t], (c + 1, h),
            )
            for t in (0, 1)
        ]

    def back(d):
        return [
            remote(piece(d, t), rel[t].at[d], sr.at[d, t], rr.at[d, t], (c - 3, h))
            for t in (0, 1)
        ]

    def onward(d, half):
        return [
            remote(
                rel[t].at[d], two[half][d // 2][t].at[rows(hx[d] % 2)],
                sf.at[d, t], r2.at[d, t], (c + 5, h),
            )
            for t in (0, 1)
        ]

    def start(copies):
        for copy in copies:
            copy.start()

    def taken(copies):
        for copy in copies:
            copy.wait_recv()

    barrier = pltpu.get_barrier_semaphore()

    def greet(device):
        pl.semaphore_signal(barrier, 1, device_id=device, device_id_type=MESH)

    for d in (1, 2, 3):
        greet((c, hx[d]))

    @pl.when(has_prev)
    def _():
        greet((c - 1, h))

    @pl.when(relays)
    def _():
        greet((c + 3, h))

    @pl.when((z == 0) & has_prev)
    def _():
        greet((c - 5, h))

    local = [
        pltpu.make_async_copy(len_hbm, lens, loc.at[0]),
        pltpu.make_async_copy(k_hbm.at[:, cols(h)], ko.at[rows(h)], loc.at[1]),
        pltpu.make_async_copy(v_hbm.at[:, cols(h)], vo.at[rows(h)], loc.at[2]),
        pltpu.make_async_copy(q_hbm, qv, loc.at[3]),
    ]
    start(local)
    others = jnp.where(has_next, 1, 0) + jnp.where(to_relay, 1, 0) + jnp.where(relays, 1, 0)
    pl.semaphore_wait(barrier, 3 + others)

    @pl.when(has_next)
    def _():
        start(first(0))

    @pl.when(to_relay)
    def _():
        start(back(0))

    for d in (1, 2, 3):
        start(exchange(d))

    @pl.when(c == 0)
    def _():
        for ref in (k1a, v1a, k1b, v1b):
            ref[...] = jnp.zeros((256, 256), BF16)

    @pl.when(c <= 1)
    def _():
        for ref in (k2h, v2h, k2l, v2l):
            ref[...] = jnp.zeros((256, 256), BF16)

    local[0].wait()
    tok = c * 512

    def later(i, carry):
        end, begin = carry
        for u in range(8):
            end = end + lens[i * 8 + u]
            begin = jnp.where(lanes >= end, end, begin)
        return end, begin

    lanes = tok + lax.broadcasted_iota(jnp.int32, (8, 512), 1)
    _, begin = lax.fori_loop(0, 8, later, (jnp.int32(0), jnp.zeros((8, 512), jnp.int32)))
    begin = begin.astype(F32)

    def masks():
        spread = lax.broadcasted_iota(jnp.int32, (128, 128), 1)
        for r in range(0, 512, 128):
            lead = jnp.tile(begin[:, r : r + 128], (16, 1)).T.astype(jnp.int32)
            pos = tok + r + lax.broadcasted_iota(jnp.int32, (128, 128), 0)
            for ref, base, size in (
                (bo, tok, 512), (b1a, tok - 512 + 256 * hh, 256), (b1b, tok - 256 - 256 * hh, 256),
                (b2h, tok - 768, 256), (b2l, tok - 1024, 256),
            ):
                if ref is b2l and r >= 256:
                    continue
                for k in range(0, size, 128):
                    key = base + k + spread
                    allowed = lead <= key
                    if ref is bo:
                        allowed = allowed & (key <= pos)
                    ref[r : r + 128, k : k + 128] = jnp.where(allowed, 0.0, NEG)

    for d in (1, 2, 3):
        taken(exchange(d))

        @pl.when(has_next)
        def _():
            start(first(d))

        @pl.when(to_relay)
        def _():
            start(back(d))

        if d == 1:
            masks()

    for copy in local[1:]:
        copy.wait()

    ones = {size: jnp.ones((size, HD), BF16) for size in (256, 512)}

    def stage(kw, vw, bias, tiles, opening=False, between=None):
        def scores(head, slot):
            shared = pl.ds(pl.multiple_of(head // 8 * HD, HD), HD)
            for r, nr, nk, _ in tiles:
                q = qv[r : r + nr, pl.ds(pl.multiple_of(head * HD, HD), HD)]
                sb[slot, r : r + nr, 0:nk] = dot(q, kw[0:nk, shared], 1, 1)

        def mix(head, slot):
            shared = pl.ds(pl.multiple_of(head // 8 * HD, HD), HD)
            for r, nr, nk, closing in tiles:
                s = sb[slot, r : r + nr, 0:nk] * SCALE + bias[r : r + nr, 0:nk]
                high = jnp.max(s, axis=1, keepdims=True)
                if opening:
                    new = jnp.broadcast_to(high, (nr, HD))
                else:
                    old = top[head, r : r + nr, :]
                    new = jnp.maximum(old, high)
                p = jnp.exp2(s - jnp.tile(new, (1, nk // HD))).astype(BF16)
                v = jnp.concatenate([vw[0:nk, shared], ones[nk]], axis=1)
                o = dot(p, v, 1, 0)
                if not opening:
                    o = acc[head, r : r + nr, :] * jnp.tile(jnp.exp2(old - new), (1, 2)) + o
                if closing:
                    out[r : r + nr, pl.ds(pl.multiple_of(head * HD, HD), HD)] = (
                        o[:, 0:HD] / o[:, HD : 2 * HD]
                    ).astype(BF16)
                else:
                    acc[head, r : r + nr, :] = o
                    top[head, r : r + nr, :] = new

        scores(0, 0)

        def step(i, carry):
            for u in range(UNROLL):
                head = i * UNROLL + u
                scores(lax.rem(head + 1, 16), (u + 1) % 2)
                mix(head, u % 2)
            if between is not None:

                @pl.when(i == 0)
                def _():
                    between()

            return carry

        lax.fori_loop(0, 16 // UNROLL, step, 0)

    def relay(d):
        @pl.when(relays)
        def _():
            taken(back(d))

        for half in (0, 1):

            @pl.when(relays & (hh == half))
            def _():
                start(onward(d, half))

    def forward(cond, half, pieces):
        @pl.when(cond & has_prev & (hh == half))
        def _():
            for d in pieces:
                if d > 1:
                    taken(first(d))

        @pl.when(cond & passes & (hh == half))
        def _():
            for d in pieces:
                start(second(d, half))

    def forward_early(cond):
        forward(cond, 0, (2,))
        forward(cond, 1, (0, 1))

    def forward_late(cond):
        forward(cond, 0, (3, 1, 0))
        forward(cond, 1, (2, 3))

    stage(ko, vo, bo, [(0, 256, 256, False), (256, 256, 512, False)], True, lambda: relay(0))
    relay(1)

    @pl.when(has_prev)
    def _():
        taken(first(0))
        taken(first(1))

    forward_early(z != 0)

    def middle():
        relay(2)
        forward_late(z != 0)
        forward_early(z == 0)

    stage(k1a, v1a, b1a, [(0, 512, 256, False)], between=middle)
    relay(3)
    forward_late(z == 0)
    stage(k1b, v1b, b1b, [(0, 512, 256, False)])

    def landed(half, pieces):
        @pl.when((c > 1) & (hh == half))
        def _():
            for d in pieces:
                taken(second(d, half))

    landed(0, (2, 3))
    landed(1, (0, 1))
    stage(k2h, v2h, b2h, [(0, 256, 256, False), (256, 256, 256, True)])
    landed(0, (0, 1))
    landed(1, (2, 3))
    stage(k2l, v2l, b2l, [(0, 256, 256, True)])

    for d in (1, 2, 3):
        for copy in exchange(d):
            copy.wait_send()
    for d in range(4):

        @pl.when(has_next)
        def _():
            for copy in first(d):
                copy.wait_send()

        @pl.when(passes)
        def _():
            for copy in second(d, 0):
                copy.wait_send()

        @pl.when(to_relay)
        def _():
            for copy in back(d):
                copy.wait_send()

        @pl.when(relays)
        def _():
            for copy in onward(d, 0):
                copy.wait_send()


def per_device(n, queries, keys, values, lengths):
    hbm = pl.BlockSpec(memory_space=pltpu.HBM)
    sems = pltpu.SemaphoreType.DMA((4, 2))
    return pl.pallas_call(
        functools.partial(kernel, n),
        out_shape=jax.ShapeDtypeStruct(queries.shape, BF16),
        in_specs=[hbm] * 4,
        out_specs=pl.BlockSpec(memory_space=pltpu.VMEM),
        scratch_shapes=[pltpu.VMEM((512, 2048), BF16)]
        + [pltpu.VMEM((512, 256), BF16)] * 2
        + [pltpu.VMEM((256, 256), BF16)] * 8
        + [pltpu.VMEM((4, 128, 256), BF16)] * 2
        + [pltpu.VMEM((512, 512), F32)]
        + [pltpu.VMEM((512, 256), F32)] * 3
        + [pltpu.VMEM((256, 256), F32)]
        + [
            pltpu.VMEM((16, 512, 256), F32),
            pltpu.VMEM((16, 512, 128), F32),
            pltpu.VMEM((2, 512, 512), F32),
            pltpu.SMEM((64,), jnp.int32),
            pltpu.SemaphoreType.DMA((4,)),
        ]
        + [sems] * 9,
        compiler_params=pltpu.CompilerParams(
            collective_id=0, has_side_effects=True, vmem_limit_bytes=58 * 2**20
        ),
    )(queries, keys, values, lengths)


def solution(mesh):
    placed = (P("ctx", "head"), P(("ctx", "head"), None), P(("ctx", "head"), None), P())
    return jax.shard_map(
        functools.partial(per_device, mesh.shape["ctx"]),
        mesh=mesh,
        in_specs=placed,
        out_specs=P("ctx", "head"),
        check_vma=False,
    )
```

```python
import functools

import jax
import jax.numpy as jnp
from jax import lax
from jax.experimental import pallas as pl
from jax.experimental.pallas import tpu as pltpu
from jax.sharding import PartitionSpec as P

HD = 128
SCALE = 128**-0.5 * 1.4426950408889634
NEG = -1e30
BF16 = jnp.bfloat16
F32 = jnp.float32
MESH = pl.DeviceIdType.MESH
PARTS = 4


def dot(a, b, ca, cb):
    return lax.dot_general(a, b, (((ca,), (cb,)), ((), ())), preferred_element_type=F32)


def kernel(
    n, q_hbm, k_hbm, v_hbm, len_hbm, out, qv, ko, vo, k1a, v1a, k1b, v1b, k2h, v2h, k21, v21, k20, v20,
    bo, b1a, b1b, b2h, b21, b20, acc, top, sb, lens, loc, a_send, a_recv, s1, r1, s2, r2, flush, ov2, ov1, ov0,
):
    c = lax.axis_index("ctx")
    h = lax.axis_index("head")
    hx = [h, (h // 2) * 2 + 1 - h % 2, (1 - h // 2) * 2 + h % 2, 3 - h]
    hh = h // 2
    z = c % 8
    has_next = c < n - 1
    has_prev = c > 0
    passes = has_prev & has_next

    def cols(g):
        return pl.ds(pl.multiple_of(g * 256, 256), 256)

    def rows(b):
        return pl.ds(pl.multiple_of(b * 128, 128), 128)

    src, own = (k_hbm, v_hbm), (ko, vo)
    one = ((k1a, v1a), (k1a, v1a), (k1b, v1b), (k1b, v1b))
    low = ((k20, v20), (k21, v21))

    def remote(a, b, send, recv, device):
        return pltpu.make_async_remote_copy(
            a, b, send, recv, device_id=device, device_id_type=MESH
        )

    def exchange(d):
        return [
            remote(src[t].at[:, cols(hx[d])], own[t].at[rows(h)], a_send.at[d, t], a_recv.at[d, t], (c, hx[d]))
            for t in (0, 1)
        ]

    def piece(d, t):
        return src[t].at[:, cols(h)] if d == 0 else own[t].at[rows(hx[d])]

    def first(d):
        return [
            remote(piece(d, t), one[d][t].at[rows(hx[d] % 2)], s1.at[d, t], r1.at[d, t], (c + 1, h))
            for t in (0, 1)
        ]

    def second(d, b=None):
        return [
            remote(
                one[d][t].at[rows(hx[d] % 2)], (k2h, v2h)[t].at[rows(hx[d] % 2)] if b is None else low[b][t],
                s2.at[d, t], r2.at[d, t], (c + 1, h),
            )
            for t in (0, 1)
        ]

    def start(copies):
        for copy in copies:
            copy.start()

    def taken(copies):
        for copy in copies:
            copy.wait_recv()

    barrier = pltpu.get_barrier_semaphore()

    def greet(device):
        pl.semaphore_signal(barrier, 1, device_id=device, device_id_type=MESH)

    for d in (1, 2, 3):
        greet((c, hx[d]))

    @pl.when(has_prev)
    def _():
        greet((c - 1, h))

    local = [
        pltpu.make_async_copy(len_hbm, lens, loc.at[0]),
        pltpu.make_async_copy(k_hbm.at[:, cols(h)], ko.at[rows(h)], loc.at[1]),
        pltpu.make_async_copy(v_hbm.at[:, cols(h)], vo.at[rows(h)], loc.at[2]),
        pltpu.make_async_copy(q_hbm, qv, loc.at[3]),
    ]
    start(local)
    pl.semaphore_wait(barrier, 3 + jnp.where(has_next, 1, 0))

    @pl.when(has_next)
    def _():
        start(first(0))

    for d in (1, 2, 3):
        start(exchange(d))

    @pl.when(c == 0)
    def _():
        for ref in (k1a, v1a, k1b, v1b):
            ref[...] = jnp.zeros((256, 256), BF16)

    @pl.when(c <= 1)
    def _():
        for ref in (k2h, v2h, k21, v21, k20, v20):
            ref[...] = jnp.zeros(ref.shape, BF16)

    local[0].wait()
    tok = c * 512

    def later(i, carry):
        end, begin = carry
        for u in range(8):
            end = end + lens[i * 8 + u]
            begin = jnp.where(lanes >= end, end, begin)
        return end, begin

    lanes = tok + lax.broadcasted_iota(jnp.int32, (8, 512), 1)
    _, begin = lax.fori_loop(0, 8, later, (jnp.int32(0), jnp.zeros((8, 512), jnp.int32)))
    begin = begin.astype(F32)

    def masks():
        spread = lax.broadcasted_iota(jnp.int32, (128, 128), 1)
        for r in range(0, 512, 128):
            lead = jnp.tile(begin[:, r : r + 128], (16, 1)).T.astype(jnp.int32)
            pos = tok + r + lax.broadcasted_iota(jnp.int32, (128, 128), 0)
            for ref, base, size in (
                (bo, tok, 512), (b1a, tok - 512 + 256 * hh, 256), (b1b, tok - 256 - 256 * hh, 256),
                (b2h, tok - 768, 256), (b21, tok - 896, 128), (b20, tok - 1024, 128),
            ):
                if (ref is b21 and r >= 256) or (ref is b20 and r >= 128):
                    continue
                for k in range(0, size, 128):
                    key = base + k + spread
                    allowed = lead <= key
                    if ref is bo:
                        allowed = allowed & (key <= pos)
                    ref[r : r + 128, k : k + 128] = jnp.where(allowed, 0.0, NEG)

    for d in (1, 2, 3):
        taken(exchange(d))

        @pl.when(has_next)
        def _():
            start(first(d))

        if d == 1:
            masks()

    for copy in local[1:]:
        copy.wait()

    ones = {size: jnp.ones((size, HD), BF16) for size in (128, 256, 512)}

    def stage(kw, vw, bias, tiles, opening=False, between=None, unroll=8):
        def scores(head, slot):
            shared = pl.ds(pl.multiple_of(head // 8 * HD, HD), HD)
            for r, nr, k, nk, _ in tiles:
                q = qv[r : r + nr, pl.ds(pl.multiple_of(head * HD, HD), HD)]
                sb[slot, r : r + nr, 0:nk] = dot(q, kw[k : k + nk, shared], 1, 1)

        def mix(head, slot):
            shared = pl.ds(pl.multiple_of(head // 8 * HD, HD), HD)
            for r, nr, k, nk, closing in tiles:
                s = sb[slot, r : r + nr, 0:nk] * SCALE + bias[r : r + nr, k : k + nk]
                high = jnp.max(s, axis=1, keepdims=True)
                if opening:
                    new = jnp.broadcast_to(high, (nr, HD))
                else:
                    old = top[head, r : r + nr, :]
                    new = jnp.maximum(old, high)
                p = jnp.exp2(s - jnp.tile(new, (1, nk // HD))).astype(BF16)
                v = jnp.concatenate([vw[k : k + nk, shared], ones[nk]], axis=1)
                o = dot(p, v, 1, 0)
                if not opening:
                    o = acc[head, r : r + nr, :] * jnp.tile(jnp.exp2(old - new), (1, 2)) + o
                if closing is not None:
                    closing[:, pl.ds(pl.multiple_of(head * HD, HD), HD)] = (
                        o[:, 0:HD] / o[:, HD : 2 * HD]
                    ).astype(BF16)
                else:
                    acc[head, r : r + nr, :] = o
                    top[head, r : r + nr, :] = new

        scores(0, 0)

        def step(i, carry):
            for u in range(unroll):
                head = i * unroll + u
                scores(lax.rem(head + 1, 16), (u + 1) % 2)
                mix(head, u % 2)
            if between is not None:

                @pl.when(i == 0)
                def _():
                    between()

            return carry

        lax.fori_loop(0, 16 // unroll, step, 0)

    def forward(cond, half, pieces):
        @pl.when(cond & has_prev & (hh == half))
        def _():
            for d in pieces:
                if d > 1:
                    taken(first(d))

        @pl.when(cond & passes & (hh == half))
        def _():
            for d in pieces:
                if d // 2 != half:
                    start(second(d))

        for b in (1, 0):
            for d in pieces:
                if d // 2 == half:

                    @pl.when(cond & passes & (hh == half) & (hx[d] == b))
                    def _():
                        start(second(d, b))

    def forward_early(cond):
        forward(cond, 0, (2,))
        forward(cond, 1, (0, 1))

    def forward_late(cond):
        forward(cond, 0, (3, 1, 0))
        forward(cond, 1, (2, 3))

    stage(ko, vo, bo, [(0, 256, 0, 256, None), (256, 256, 0, 512, None)], True)

    @pl.when(has_prev)
    def _():
        taken(first(0))
        taken(first(1))

    forward_early(z != 0)

    def middle():
        forward_late(z != 0)
        forward_early(z == 0)

    stage(k1a, v1a, b1a, [(0, 512, 0, 256, None)], between=middle)
    forward_late(z == 0)
    stage(k1b, v1b, b1b, [(0, 512, 0, 256, None)])

    def landed(half, pieces):
        @pl.when((c > 1) & (hh == half))
        def _():
            for d in pieces:
                taken(second(d))

    def landed_low(b):
        for half in (0, 1):
            for d in (2 * half, 2 * half + 1):

                @pl.when((c > 1) & (hh == half) & (hx[d] == b))
                def _():
                    taken(second(d, b))

    def flushed(i, ref, r):
        return pltpu.make_async_copy(ref, out.at[r : r + ref.shape[0]], flush.at[i])

    landed(0, (2, 3))
    landed(1, (0, 1))
    stage(k2h, v2h, b2h, [(0, 256, 0, 256, None), (256, 256, 0, 256, ov2)])
    flushed(0, ov2, 256).start()
    landed_low(1)
    stage(k21, v21, b21, [(0, 128, 0, 128, None), (128, 128, 0, 128, ov1)], unroll=16)
    flushed(1, ov1, 128).start()
    landed_low(0)
    stage(k20, v20, b20, [(0, 128, 0, 128, ov0)], unroll=16)
    flushed(2, ov0, 0).start()

    for d in (1, 2, 3):
        for copy in exchange(d):
            copy.wait_send()
    flushed(0, ov2, 256).wait()
    flushed(1, ov1, 128).wait()
    flushed(2, ov0, 0).wait()
    for d in range(4):

        @pl.when(has_next)
        def _():
            for copy in first(d):
                copy.wait_send()

        @pl.when(passes)
        def _():
            for copy in second(d):
                copy.wait_send()


def place(a, b, held, came, went):
    size = a.shape[0] // PARTS

    def part(ref, i):
        return ref.at[pl.ds(i * size, size)]

    come = [pltpu.make_async_copy(part(a, i), part(held, i), came.at[i]) for i in range(PARTS)]
    go = [pltpu.make_async_copy(part(held, i), part(b, i), went.at[i]) for i in range(PARTS)]
    for copy in come:
        copy.start()
    for i in range(PARTS):
        come[i].wait()
        go[i].start()
    for copy in go:
        copy.wait()


def per_device(n, queries, keys, values, lengths):
    hbm = pl.BlockSpec(memory_space=pltpu.HBM)
    sems = pltpu.SemaphoreType.DMA((4, 2))
    attended = pl.pallas_call(
        functools.partial(kernel, n),
        out_shape=jax.ShapeDtypeStruct(queries.shape, BF16),
        in_specs=[hbm] * 4,
        out_specs=hbm,
        scratch_shapes=[pltpu.VMEM((512, 2048), BF16)]
        + [pltpu.VMEM((512, 256), BF16)] * 2
        + [pltpu.VMEM((256, 256), BF16)] * 6
        + [pltpu.VMEM((128, 256), BF16)] * 4
        + [pltpu.VMEM((512, 512), F32)]
        + [pltpu.VMEM((512, 256), F32)] * 3
        + [pltpu.VMEM((256, 128), F32), pltpu.VMEM((128, 128), F32)]
        + [
            pltpu.VMEM((16, 512, 256), F32),
            pltpu.VMEM((16, 512, 128), F32),
            pltpu.VMEM((2, 512, 512), F32),
            pltpu.SMEM((64,), jnp.int32),
            pltpu.SemaphoreType.DMA((4,)),
        ]
        + [sems] * 6
        + [pltpu.SemaphoreType.DMA((3,)), pltpu.VMEM((256, 2048), BF16)]
        + [pltpu.VMEM((128, 2048), BF16)] * 2,
        compiler_params=pltpu.CompilerParams(
            collective_id=0, has_side_effects=True, vmem_limit_bytes=58 * 2**20
        ),
    )(queries, keys, values, lengths)
    return pl.pallas_call(
        place,
        out_shape=jax.ShapeDtypeStruct(queries.shape, BF16),
        in_specs=[hbm],
        out_specs=hbm,
        scratch_shapes=[pltpu.VMEM(queries.shape, BF16)] + [pltpu.SemaphoreType.DMA((PARTS,))] * 2,
    )(attended)


def solution(mesh):
    placed = (P("ctx", "head"), P(("ctx", "head"), None), P(("ctx", "head"), None), P())
    return jax.shard_map(
        functools.partial(per_device, mesh.shape["ctx"]),
        mesh=mesh,
        in_specs=placed,
        out_specs=P("ctx", "head"),
        check_vma=False,
    )
```

```python
import functools

import jax
import jax.numpy as jnp
from jax import lax
from jax.experimental import pallas as pl
from jax.experimental.pallas import tpu as pltpu
from jax.sharding import PartitionSpec as P

HD = 128
SCALE = 128**-0.5 * 1.4426950408889634
NEG = -1e30
BF16 = jnp.bfloat16
F32 = jnp.float32
MESH = pl.DeviceIdType.MESH
PARTS = 4


def dot(a, b, ca, cb):
    return lax.dot_general(a, b, (((ca,), (cb,)), ((), ())), preferred_element_type=F32)


def kernel(
    n, q_hbm, k_hbm, v_hbm, len_hbm, out, qv, ko, vo, k1a, v1a, k1b, v1b, k2p, v2p, k2q, v2q, k21, v21, k20, v20,
    bo, b1a, b1b, b2p, b2q, b21, b20, acc, top, sb, lens, loc, a_send, a_recv, s1, r1, s2, r2, flush, ov2, ov1, ov0,
):
    c = lax.axis_index("ctx")
    h = lax.axis_index("head")
    hx = [h, (h // 2) * 2 + 1 - h % 2, (1 - h // 2) * 2 + h % 2, 3 - h]
    hh = h // 2
    z = c % 8
    has_next = c < n - 1
    has_prev = c > 0
    passes = has_prev & has_next

    def cols(g):
        return pl.ds(pl.multiple_of(g * 256, 256), 256)

    def rows(b):
        return pl.ds(pl.multiple_of(b * 128, 128), 128)

    src, own = (k_hbm, v_hbm), (ko, vo)
    one = ((k1a, v1a), (k1a, v1a), (k1b, v1b), (k1b, v1b))
    low = ((k20, v20), (k21, v21))
    high = ((k2p, v2p), (k2q, v2q))

    def remote(a, b, send, recv, device):
        return pltpu.make_async_remote_copy(
            a, b, send, recv, device_id=device, device_id_type=MESH
        )

    def exchange(d):
        return [
            remote(src[t].at[:, cols(hx[d])], own[t].at[rows(h)], a_send.at[d, t], a_recv.at[d, t], (c, hx[d]))
            for t in (0, 1)
        ]

    def piece(d, t):
        return src[t].at[:, cols(h)] if d == 0 else own[t].at[rows(hx[d])]

    def first(d):
        return [
            remote(piece(d, t), one[d][t].at[rows(hx[d] % 2)], s1.at[d, t], r1.at[d, t], (c + 1, h))
            for t in (0, 1)
        ]

    def second(d, b=None):
        return [
            remote(
                one[d][t].at[rows(hx[d] % 2)], high[d % 2][t] if b is None else low[b][t],
                s2.at[d, t], r2.at[d, t], (c + 1, h),
            )
            for t in (0, 1)
        ]

    def start(copies):
        for copy in copies:
            copy.start()

    def taken(copies):
        for copy in copies:
            copy.wait_recv()

    barrier = pltpu.get_barrier_semaphore()

    def greet(device):
        pl.semaphore_signal(barrier, 1, device_id=device, device_id_type=MESH)

    for d in (1, 2, 3):
        greet((c, hx[d]))

    @pl.when(has_prev)
    def _():
        greet((c - 1, h))

    local = [
        pltpu.make_async_copy(len_hbm, lens, loc.at[0]),
        pltpu.make_async_copy(k_hbm.at[:, cols(h)], ko.at[rows(h)], loc.at[1]),
        pltpu.make_async_copy(v_hbm.at[:, cols(h)], vo.at[rows(h)], loc.at[2]),
        pltpu.make_async_copy(q_hbm, qv, loc.at[3]),
    ]
    start(local)
    pl.semaphore_wait(barrier, 3 + jnp.where(has_next, 1, 0))

    @pl.when(has_next)
    def _():
        start(first(0))

    for d in (1, 2, 3):
        start(exchange(d))

    @pl.when(c == 0)
    def _():
        for ref in (k1a, v1a, k1b, v1b):
            ref[...] = jnp.zeros((256, 256), BF16)

    @pl.when(c <= 1)
    def _():
        for ref in (k2p, v2p, k2q, v2q, k21, v21, k20, v20):
            ref[...] = jnp.zeros(ref.shape, BF16)

    local[0].wait()
    tok = c * 512

    def later(i, carry):
        end, begin = carry
        for u in range(8):
            end = end + lens[i * 8 + u]
            begin = jnp.where(lanes >= end, end, begin)
        return end, begin

    lanes = tok + lax.broadcasted_iota(jnp.int32, (8, 512), 1)
    _, begin = lax.fori_loop(0, 8, later, (jnp.int32(0), jnp.zeros((8, 512), jnp.int32)))
    begin = begin.astype(F32)

    def masks():
        spread = lax.broadcasted_iota(jnp.int32, (128, 128), 1)
        for r in range(0, 512, 128):
            lead = jnp.tile(begin[:, r : r + 128], (16, 1)).T.astype(jnp.int32)
            pos = tok + r + lax.broadcasted_iota(jnp.int32, (128, 128), 0)
            for ref, base, size in (
                (bo, tok, 512), (b1a, tok - 512 + 256 * hh, 256), (b1b, tok - 256 - 256 * hh, 256),
                (b2p, tok - 768 + 128 * (h % 2), 128), (b2q, tok - 640 - 128 * (h % 2), 128), (b21, tok - 896, 128), (b20, tok - 1024, 128),
            ):
                if (ref is b21 and r >= 256) or (ref is b20 and r >= 128):
                    continue
                for k in range(0, size, 128):
                    key = base + k + spread
                    allowed = lead <= key
                    if ref is bo:
                        allowed = allowed & (key <= pos)
                    ref[r : r + 128, k : k + 128] = jnp.where(allowed, 0.0, NEG)

    for d in (1, 2, 3):
        taken(exchange(d))

        @pl.when(has_next)
        def _():
            start(first(d))

        if d == 1:
            masks()

    for copy in local[1:]:
        copy.wait()

    ones = {size: jnp.ones((size, HD), BF16) for size in (128, 256, 512)}

    def stage(kw, vw, bias, tiles, opening=False, between=None, unroll=8):
        def scores(head, slot):
            shared = pl.ds(pl.multiple_of(head // 8 * HD, HD), HD)
            for r, nr, k, nk, _ in tiles:
                q = qv[r : r + nr, pl.ds(pl.multiple_of(head * HD, HD), HD)]
                sb[slot, r : r + nr, 0:nk] = dot(q, kw[k : k + nk, shared], 1, 1)

        def mix(head, slot):
            shared = pl.ds(pl.multiple_of(head // 8 * HD, HD), HD)
            for r, nr, k, nk, closing in tiles:
                s = sb[slot, r : r + nr, 0:nk] * SCALE + bias[r : r + nr, k : k + nk]
                high = jnp.max(s, axis=1, keepdims=True)
                if opening:
                    new = jnp.broadcast_to(high, (nr, HD))
                else:
                    old = top[head, r : r + nr, :]
                    new = jnp.maximum(old, high)
                p = jnp.exp2(s - jnp.tile(new, (1, nk // HD))).astype(BF16)
                v = jnp.concatenate([vw[k : k + nk, shared], ones[nk]], axis=1)
                o = dot(p, v, 1, 0)
                if not opening:
                    o = acc[head, r : r + nr, :] * jnp.tile(jnp.exp2(old - new), (1, 2)) + o
                keep = nr
                if closing is not None:
                    ref, keep = closing
                    ref[:, pl.ds(pl.multiple_of(head * HD, HD), HD)] = (
                        o[keep:, 0:HD] / o[keep:, HD : 2 * HD]
                    ).astype(BF16)
                if keep:
                    acc[head, r : r + keep, :] = o[:keep]
                    top[head, r : r + keep, :] = new[:keep]

        scores(0, 0)

        def step(i, carry):
            for u in range(unroll):
                head = i * unroll + u
                scores(lax.rem(head + 1, 16), (u + 1) % 2)
                mix(head, u % 2)
            if between is not None:

                @pl.when(i == 0)
                def _():
                    between()

            return carry

        lax.fori_loop(0, 16 // unroll, step, 0)

    def forward(cond, half, pieces):
        @pl.when(cond & has_prev & (hh == half))
        def _():
            for d in pieces:
                if d > 1:
                    taken(first(d))

        @pl.when(cond & passes & (hh == half))
        def _():
            for d in pieces:
                if d // 2 != half:
                    start(second(d))

        for b in (1, 0):
            for d in pieces:
                if d // 2 == half:

                    @pl.when(cond & passes & (hh == half) & (hx[d] == b))
                    def _():
                        start(second(d, b))

    def forward_early(cond):
        forward(cond, 0, (2,))
        forward(cond, 1, (0, 1))

    def forward_late(cond):
        forward(cond, 0, (3, 1, 0))
        forward(cond, 1, (2, 3))

    def take_first(cond):
        @pl.when(has_prev & cond)
        def _():
            taken(first(0))
            taken(first(1))

    def early():
        take_first(z != 0)
        forward_early(z != 0)

    stage(ko, vo, bo, [(0, 256, 0, 256, None), (256, 256, 0, 512, None)], True, early)
    take_first(z == 0)
    forward_late(z != 0)
    stage(k1a, v1a, b1a, [(0, 512, 0, 256, None)], between=lambda: forward_early(z == 0))
    forward_late(z == 0)
    stage(k1b, v1b, b1b, [(0, 512, 0, 256, None)])

    def landed(half, d):
        @pl.when((c > 1) & (hh == half))
        def _():
            taken(second(d))

    def landed_low(b):
        for half in (0, 1):
            for d in (2 * half, 2 * half + 1):

                @pl.when((c > 1) & (hh == half) & (hx[d] == b))
                def _():
                    taken(second(d, b))

    def flushed(i, ref, r):
        return pltpu.make_async_copy(ref, out.at[r : r + ref.shape[0]], flush.at[i])

    landed(0, 2)
    landed(1, 0)
    stage(k2p, v2p, b2p, [(0, 512, 0, 128, None)])
    landed(0, 3)
    landed(1, 1)
    stage(k2q, v2q, b2q, [(0, 512, 0, 128, (ov2, 256))])
    flushed(0, ov2, 256).start()
    landed_low(1)
    stage(k21, v21, b21, [(0, 256, 0, 128, (ov1, 128))], unroll=16)
    flushed(1, ov1, 128).start()
    landed_low(0)
    stage(k20, v20, b20, [(0, 128, 0, 128, (ov0, 0))], unroll=16)
    flushed(2, ov0, 0).start()

    for d in (1, 2, 3):
        for copy in exchange(d):
            copy.wait_send()
    flushed(0, ov2, 256).wait()
    flushed(1, ov1, 128).wait()
    flushed(2, ov0, 0).wait()
    for d in range(4):

        @pl.when(has_next)
        def _():
            for copy in first(d):
                copy.wait_send()

        @pl.when(passes)
        def _():
            for copy in second(d):
                copy.wait_send()


def place(a, b, held, came, went):
    size = a.shape[0] // PARTS

    def part(ref, i):
        return ref.at[pl.ds(i * size, size)]

    come = [pltpu.make_async_copy(part(a, i), part(held, i), came.at[i]) for i in range(PARTS)]
    go = [pltpu.make_async_copy(part(held, i), part(b, i), went.at[i]) for i in range(PARTS)]
    for copy in come:
        copy.start()
    for i in range(PARTS):
        come[i].wait()
        go[i].start()
    for copy in go:
        copy.wait()


def per_device(n, queries, keys, values, lengths):
    hbm = pl.BlockSpec(memory_space=pltpu.HBM)
    sems = pltpu.SemaphoreType.DMA((4, 2))
    attended = pl.pallas_call(
        functools.partial(kernel, n),
        out_shape=jax.ShapeDtypeStruct(queries.shape, BF16),
        in_specs=[hbm] * 4,
        out_specs=hbm,
        scratch_shapes=[pltpu.VMEM((512, 2048), BF16)]
        + [pltpu.VMEM((512, 256), BF16)] * 2
        + [pltpu.VMEM((256, 256), BF16)] * 4
        + [pltpu.VMEM((128, 256), BF16)] * 8
        + [pltpu.VMEM((512, 512), F32)]
        + [pltpu.VMEM((512, 256), F32)] * 2
        + [pltpu.VMEM((512, 128), F32)] * 2
        + [pltpu.VMEM((256, 128), F32), pltpu.VMEM((128, 128), F32)]
        + [
            pltpu.VMEM((16, 512, 256), F32),
            pltpu.VMEM((16, 512, 128), F32),
            pltpu.VMEM((2, 512, 512), F32),
            pltpu.SMEM((64,), jnp.int32),
            pltpu.SemaphoreType.DMA((4,)),
        ]
        + [sems] * 6
        + [pltpu.SemaphoreType.DMA((3,)), pltpu.VMEM((256, 2048), BF16)]
        + [pltpu.VMEM((128, 2048), BF16)] * 2,
        compiler_params=pltpu.CompilerParams(
            collective_id=0, has_side_effects=True, vmem_limit_bytes=58 * 2**20
        ),
    )(queries, keys, values, lengths)
    return jnp.where(lengths[0] > 0, attended, jnp.zeros_like(attended))


def solution(mesh):
    placed = (P("ctx", "head"), P(("ctx", "head"), None), P(("ctx", "head"), None), P())
    return jax.shard_map(
        functools.partial(per_device, mesh.shape["ctx"]),
        mesh=mesh,
        in_specs=placed,
        out_specs=P("ctx", "head"),
        check_vma=False,
    )
```

```python
import functools

import jax
import jax.numpy as jnp
from jax import lax
from jax.experimental import pallas as pl
from jax.experimental.pallas import tpu as pltpu
from jax.sharding import PartitionSpec as P

HD = 128
SCALE = 128**-0.5 * 1.4426950408889634
NEG = -1e30
BF16 = jnp.bfloat16
F32 = jnp.float32
MESH = pl.DeviceIdType.MESH
PARTS = 4


def dot(a, b, ca, cb):
    return lax.dot_general(a, b, (((ca,), (cb,)), ((), ())), preferred_element_type=F32)


def kernel(
    n, q_hbm, k_hbm, v_hbm, len_hbm, out, qv, ko, vo, k1a, v1a, k1b, v1b, k2p, v2p, k2q, v2q, k21, v21, k20, v20,
    bo, b1a, b1b, b2p, b2q, b21, b20, acc, top, sb, lens, loc, a_send, a_recv, s1, r1, s2, r2, flush, ov2, ov1, ov0,
):
    c = lax.axis_index("ctx")
    h = lax.axis_index("head")
    hx = [h, (h // 2) * 2 + 1 - h % 2, (1 - h // 2) * 2 + h % 2, 3 - h]
    hh = h // 2
    z = c % 8
    has_next = c < n - 1
    has_prev = c > 0
    passes = has_prev & has_next

    def cols(g):
        return pl.ds(pl.multiple_of(g * 256, 256), 256)

    def rows(b):
        return pl.ds(pl.multiple_of(b * 128, 128), 128)

    src, own = (k_hbm, v_hbm), (ko, vo)
    one = ((k1a, v1a), (k1a, v1a), (k1b, v1b), (k1b, v1b))
    low = ((k20, v20), (k21, v21))
    high = ((k2p, v2p), (k2q, v2q))

    def remote(a, b, send, recv, device):
        return pltpu.make_async_remote_copy(
            a, b, send, recv, device_id=device, device_id_type=MESH
        )

    def exchange(d):
        return [
            remote(src[t].at[:, cols(hx[d])], own[t].at[rows(h)], a_send.at[d, t], a_recv.at[d, t], (c, hx[d]))
            for t in (0, 1)
        ]

    def piece(d, t):
        return src[t].at[:, cols(h)] if d == 0 else own[t].at[rows(hx[d])]

    def first(d):
        return [
            remote(piece(d, t), one[d][t].at[rows(hx[d] % 2)], s1.at[d, t], r1.at[d, t], (c + 1, h))
            for t in (0, 1)
        ]

    def second(d, b=None):
        return [
            remote(
                one[d][t].at[rows(hx[d] % 2)], high[d % 2][t] if b is None else low[b][t],
                s2.at[d, t], r2.at[d, t], (c + 1, h),
            )
            for t in (0, 1)
        ]

    def start(copies):
        for copy in copies:
            copy.start()

    def taken(copies):
        for copy in copies:
            copy.wait_recv()

    barrier = pltpu.get_barrier_semaphore()

    def greet(device):
        pl.semaphore_signal(barrier, 1, device_id=device, device_id_type=MESH)

    for d in (1, 2, 3):
        greet((c, hx[d]))

    @pl.when(has_prev)
    def _():
        greet((c - 1, h))

    local = [
        pltpu.make_async_copy(len_hbm, lens, loc.at[0]),
        pltpu.make_async_copy(k_hbm.at[:, cols(h)], ko.at[rows(h)], loc.at[1]),
        pltpu.make_async_copy(v_hbm.at[:, cols(h)], vo.at[rows(h)], loc.at[2]),
        pltpu.make_async_copy(q_hbm, qv, loc.at[3]),
    ]
    start(local)
    pl.semaphore_wait(barrier, 3 + jnp.where(has_next, 1, 0))

    @pl.when(has_next)
    def _():
        start(first(0))

    for d in (1, 2, 3):
        start(exchange(d))

    @pl.when(c == 0)
    def _():
        for ref in (k1a, v1a, k1b, v1b):
            ref[...] = jnp.zeros((256, 256), BF16)

    @pl.when(c <= 1)
    def _():
        for ref in (k2p, v2p, k2q, v2q, k21, v21, k20, v20):
            ref[...] = jnp.zeros(ref.shape, BF16)

    local[0].wait()
    tok = c * 512

    def later(i, carry):
        end, begin = carry
        for u in range(8):
            end = end + lens[i * 8 + u]
            begin = jnp.where(lanes >= end, end, begin)
        return end, begin

    lanes = tok + lax.broadcasted_iota(jnp.int32, (8, 512), 1)
    _, begin = lax.fori_loop(0, 8, later, (jnp.int32(0), jnp.zeros((8, 512), jnp.int32)))
    begin = begin.astype(F32)

    def masks():
        spread = lax.broadcasted_iota(jnp.int32, (128, 128), 1)
        for r in range(0, 512, 128):
            lead = jnp.tile(begin[:, r : r + 128], (16, 1)).T.astype(jnp.int32)
            pos = tok + r + lax.broadcasted_iota(jnp.int32, (128, 128), 0)
            for ref, base, size in (
                (bo, tok, 512), (b1a, tok - 512 + 256 * hh, 256), (b1b, tok - 256 - 256 * hh, 256),
                (b2p, tok - 768 + 128 * (h % 2), 128), (b2q, tok - 640 - 128 * (h % 2), 128), (b21, tok - 896, 128), (b20, tok - 1024, 128),
            ):
                if (ref is b21 and r >= 256) or (ref is b20 and r >= 128):
                    continue
                for k in range(0, size, 128):
                    key = base + k + spread
                    allowed = lead <= key
                    if ref is bo:
                        allowed = allowed & (key <= pos)
                    ref[r : r + 128, k : k + 128] = jnp.where(allowed, 0.0, NEG)

    for d in (1, 2, 3):
        taken(exchange(d))

        @pl.when(has_next)
        def _():
            start(first(d))

        if d == 1:
            masks()

    for copy in local[1:]:
        copy.wait()

    ones = {size: jnp.ones((size, HD), BF16) for size in (128, 256, 512)}

    def stage(kw, vw, bias, tiles, opening=False, between=None, unroll=8):
        def scores(head, slot):
            shared = pl.ds(pl.multiple_of(head // 8 * HD, HD), HD)
            for r, nr, k, nk, _ in tiles:
                q = qv[r : r + nr, pl.ds(pl.multiple_of(head * HD, HD), HD)]
                sb[slot, r : r + nr, 0:nk] = dot(q, kw[k : k + nk, shared], 1, 1)

        def mix(head, slot):
            shared = pl.ds(pl.multiple_of(head // 8 * HD, HD), HD)
            for r, nr, k, nk, closing in tiles:
                s = sb[slot, r : r + nr, 0:nk] * SCALE + bias[r : r + nr, k : k + nk]
                high = jnp.max(s, axis=1, keepdims=True)
                if opening:
                    new = jnp.broadcast_to(high, (nr, HD))
                else:
                    old = top[head, r : r + nr, :]
                    new = jnp.maximum(old, high)
                p = jnp.exp2(s - jnp.tile(new, (1, nk // HD))).astype(BF16)
                v = jnp.concatenate([vw[k : k + nk, shared], ones[nk]], axis=1)
                o = dot(p, v, 1, 0)
                if not opening:
                    o = acc[head, r : r + nr, :] * jnp.tile(jnp.exp2(old - new), (1, 2)) + o
                keep = nr
                if closing is not None:
                    ref, keep = closing
                    ref[:, pl.ds(pl.multiple_of(head * HD, HD), HD)] = (
                        o[keep:, 0:HD] / o[keep:, HD : 2 * HD]
                    ).astype(BF16)
                if keep:
                    acc[head, r : r + keep, :] = o[:keep]
                    top[head, r : r + keep, :] = new[:keep]

        scores(0, 0)

        def step(i, carry):
            for u in range(unroll):
                head = i * unroll + u
                scores(lax.rem(head + 1, 16), (u + 1) % 2)
                mix(head, u % 2)
            if between is not None:

                @pl.when(i == 0)
                def _():
                    between()

            return carry

        lax.fori_loop(0, 16 // unroll, step, 0)

    def forward(cond, half, pieces):
        @pl.when(cond & has_prev & (hh == half))
        def _():
            for d in pieces:
                if d > 1:
                    taken(first(d))

        @pl.when(cond & passes & (hh == half))
        def _():
            for d in pieces:
                if d // 2 != half:
                    start(second(d))

        for b in (1, 0):
            for d in pieces:
                if d // 2 == half:

                    @pl.when(cond & passes & (hh == half) & (hx[d] == b))
                    def _():
                        start(second(d, b))

    def forward_early(cond):
        forward(cond, 0, (2,))
        forward(cond, 1, (0, 1))

    def forward_late(cond):
        forward(cond, 0, (3, 1, 0))
        forward(cond, 1, (2, 3))

    def take_first(cond):
        @pl.when(has_prev & cond)
        def _():
            taken(first(0))
            taken(first(1))

    def early():
        take_first(z != 0)
        forward_early(z != 0)

    stage(ko, vo, bo, [(0, 256, 0, 256, None), (256, 256, 0, 512, None)], True, early)
    take_first(z == 0)
    forward_late(z != 0)
    stage(k1a, v1a, b1a, [(0, 512, 0, 256, None)], between=lambda: forward_early(z == 0))
    forward_late(z == 0)
    stage(k1b, v1b, b1b, [(0, 512, 0, 256, None)])

    def landed(half, d):
        @pl.when((c > 1) & (hh == half))
        def _():
            taken(second(d))

    def landed_low(b):
        for half in (0, 1):
            for d in (2 * half, 2 * half + 1):

                @pl.when((c > 1) & (hh == half) & (hx[d] == b))
                def _():
                    taken(second(d, b))

    def flushed(i, ref, r):
        return pltpu.make_async_copy(ref, out.at[r : r + ref.shape[0]], flush.at[i])

    landed(0, 2)
    landed(1, 0)
    stage(k2p, v2p, b2p, [(0, 512, 0, 128, None)])
    landed(0, 3)
    landed(1, 1)
    stage(k2q, v2q, b2q, [(0, 512, 0, 128, (ov2, 256))])
    flushed(0, ov2, 256).start()
    landed_low(1)
    stage(k21, v21, b21, [(0, 256, 0, 128, (ov1, 128))], unroll=16)
    flushed(1, ov1, 128).start()
    for d in (1, 2, 3):
        for copy in exchange(d):
            copy.wait_send()
    for d in range(4):

        @pl.when(has_next)
        def _():
            for copy in first(d):
                copy.wait_send()

    flushed(0, ov2, 256).wait()
    landed_low(0)
    stage(k20, v20, b20, [(0, 128, 0, 128, (ov0, 0))], unroll=16)
    flushed(2, ov0, 0).start()

    flushed(1, ov1, 128).wait()
    flushed(2, ov0, 0).wait()
    for d in range(4):

        @pl.when(passes)
        def _():
            for copy in second(d):
                copy.wait_send()


def place(a, b, held, came, went):
    size = a.shape[0] // PARTS

    def part(ref, i):
        return ref.at[pl.ds(i * size, size)]

    come = [pltpu.make_async_copy(part(a, i), part(held, i), came.at[i]) for i in range(PARTS)]
    go = [pltpu.make_async_copy(part(held, i), part(b, i), went.at[i]) for i in range(PARTS)]
    for copy in come:
        copy.start()
    for i in range(PARTS):
        come[i].wait()
        go[i].start()
    for copy in go:
        copy.wait()


def per_device(n, queries, keys, values, lengths):
    hbm = pl.BlockSpec(memory_space=pltpu.HBM)
    sems = pltpu.SemaphoreType.DMA((4, 2))
    attended = pl.pallas_call(
        functools.partial(kernel, n),
        out_shape=jax.ShapeDtypeStruct(queries.shape, BF16),
        in_specs=[hbm] * 4,
        out_specs=hbm,
        scratch_shapes=[pltpu.VMEM((512, 2048), BF16)]
        + [pltpu.VMEM((512, 256), BF16)] * 2
        + [pltpu.VMEM((256, 256), BF16)] * 4
        + [pltpu.VMEM((128, 256), BF16)] * 8
        + [pltpu.VMEM((512, 512), F32)]
        + [pltpu.VMEM((512, 256), F32)] * 2
        + [pltpu.VMEM((512, 128), F32)] * 2
        + [pltpu.VMEM((256, 128), F32), pltpu.VMEM((128, 128), F32)]
        + [
            pltpu.VMEM((16, 512, 256), F32),
            pltpu.VMEM((16, 512, 128), F32),
            pltpu.VMEM((2, 512, 512), F32),
            pltpu.SMEM((64,), jnp.int32),
            pltpu.SemaphoreType.DMA((4,)),
        ]
        + [sems] * 6
        + [pltpu.SemaphoreType.DMA((3,)), pltpu.VMEM((256, 2048), BF16)]
        + [pltpu.VMEM((128, 2048), BF16)] * 2,
        compiler_params=pltpu.CompilerParams(
            collective_id=0, has_side_effects=True, vmem_limit_bytes=58 * 2**20
        ),
    )(queries, keys, values, lengths)
    return pl.pallas_call(
        place,
        out_shape=jax.ShapeDtypeStruct(queries.shape, BF16),
        in_specs=[hbm],
        out_specs=hbm,
        scratch_shapes=[pltpu.VMEM(queries.shape, BF16)] + [pltpu.SemaphoreType.DMA((PARTS,))] * 2,
    )(attended)


def solution(mesh):
    placed = (P("ctx", "head"), P(("ctx", "head"), None), P(("ctx", "head"), None), P())
    return jax.shard_map(
        functools.partial(per_device, mesh.shape["ctx"]),
        mesh=mesh,
        in_specs=placed,
        out_specs=P("ctx", "head"),
        check_vma=False,
    )
```

```python
import functools

import jax
import jax.numpy as jnp
from jax import lax
from jax.experimental import pallas as pl
from jax.experimental.pallas import tpu as pltpu
from jax.sharding import PartitionSpec as P

HD = 128
SCALE = 128**-0.5 * 1.4426950408889634
NEG = -1e30
BF16 = jnp.bfloat16
F32 = jnp.float32
MESH = pl.DeviceIdType.MESH
PARTS = 4


def dot(a, b, ca, cb):
    return lax.dot_general(a, b, (((ca,), (cb,)), ((), ())), preferred_element_type=F32)


def kernel(
    n, q_hbm, k_hbm, v_hbm, len_hbm, out, qv, ko, vo, k1a, v1a, k1b, v1b, k2p, v2p, k2q, v2q, k21, v21, k20, v20,
    bo, b1a, b1b, b2p, b2q, b21, b20, acc, top, sb, lens, loc, a_send, a_recv, s1, r1, s2, r2, flush, ov2, ov1, ov0,
):
    c = lax.axis_index("ctx")
    h = lax.axis_index("head")
    hx = [h, (h // 2) * 2 + 1 - h % 2, (1 - h // 2) * 2 + h % 2, 3 - h]
    hh = h // 2
    z = c % 8
    has_next = c < n - 1
    has_prev = c > 0
    passes = has_prev & has_next

    def cols(g):
        return pl.ds(pl.multiple_of(g * 256, 256), 256)

    def rows(b):
        return pl.ds(pl.multiple_of(b * 128, 128), 128)

    src, own = (k_hbm, v_hbm), (ko, vo)
    one = ((k1a, v1a), (k1a, v1a), (k1b, v1b), (k1b, v1b))
    low = ((k20, v20), (k21, v21))
    high = ((k2p, v2p), (k2q, v2q))

    def remote(a, b, send, recv, device):
        return pltpu.make_async_remote_copy(
            a, b, send, recv, device_id=device, device_id_type=MESH
        )

    def exchange(d):
        return [
            remote(src[t].at[:, cols(hx[d])], own[t].at[rows(h)], a_send.at[d, t], a_recv.at[d, t], (c, hx[d]))
            for t in (0, 1)
        ]

    def piece(d, t):
        return src[t].at[:, cols(h)] if d == 0 else own[t].at[rows(hx[d])]

    def first(d):
        return [
            remote(piece(d, t), one[d][t].at[rows(hx[d] % 2)], s1.at[d, t], r1.at[d, t], (c + 1, h))
            for t in (0, 1)
        ]

    def second(d, b=None):
        return [
            remote(
                one[d][t].at[rows(hx[d] % 2)], high[d % 2][t] if b is None else low[b][t],
                s2.at[d, t], r2.at[d, t], (c + 1, h),
            )
            for t in (0, 1)
        ]

    def start(copies):
        for copy in copies:
            copy.start()

    def taken(copies):
        for copy in copies:
            copy.wait_recv()

    barrier = pltpu.get_barrier_semaphore()

    def greet(device):
        pl.semaphore_signal(barrier, 1, device_id=device, device_id_type=MESH)

    @pl.when(has_prev)
    def _():
        greet((c - 1, h))

    for d in (1, 2, 3):
        greet((c, hx[d]))

    local = [
        pltpu.make_async_copy(len_hbm, lens, loc.at[0]),
        pltpu.make_async_copy(k_hbm.at[:, cols(h)], ko.at[rows(h)], loc.at[1]),
        pltpu.make_async_copy(v_hbm.at[:, cols(h)], vo.at[rows(h)], loc.at[2]),
        pltpu.make_async_copy(q_hbm, qv, loc.at[3]),
    ]
    start(local)
    local[0].wait()
    tok = c * 512

    def later(i, carry):
        end, begin = carry
        for u in range(8):
            end = end + lens[i * 8 + u]
            begin = jnp.where(lanes >= end, end, begin)
        return end, begin

    lanes = tok + lax.broadcasted_iota(jnp.int32, (8, 512), 1)
    _, begin = lax.fori_loop(0, 8, later, (jnp.int32(0), jnp.zeros((8, 512), jnp.int32)))
    begin = begin.astype(F32)

    pl.semaphore_wait(barrier, 3 + jnp.where(has_next, 1, 0))

    @pl.when(has_next)
    def _():
        start(first(0))

    for d in (1, 2, 3):
        start(exchange(d))

    @pl.when(c == 0)
    def _():
        for ref in (k1a, v1a, k1b, v1b):
            ref[...] = jnp.zeros((256, 256), BF16)

    @pl.when(c <= 1)
    def _():
        for ref in (k2p, v2p, k2q, v2q, k21, v21, k20, v20):
            ref[...] = jnp.zeros(ref.shape, BF16)

    def masks():
        spread = lax.broadcasted_iota(jnp.int32, (128, 128), 1)
        for r in range(0, 512, 128):
            lead = jnp.tile(begin[:, r : r + 128], (16, 1)).T.astype(jnp.int32)
            pos = tok + r + lax.broadcasted_iota(jnp.int32, (128, 128), 0)
            for ref, base, size in (
                (bo, tok, 512), (b1a, tok - 512 + 256 * hh, 256), (b1b, tok - 256 - 256 * hh, 256),
                (b2p, tok - 768 + 128 * (h % 2), 128), (b2q, tok - 640 - 128 * (h % 2), 128), (b21, tok - 896, 128), (b20, tok - 1024, 128),
            ):
                if (ref is b21 and r >= 256) or (ref is b20 and r >= 128):
                    continue
                for k in range(0, size, 128):
                    key = base + k + spread
                    allowed = lead <= key
                    if ref is bo:
                        allowed = allowed & (key <= pos)
                    ref[r : r + 128, k : k + 128] = jnp.where(allowed, 0.0, NEG)

    for d in (1, 2, 3):
        taken(exchange(d))

        @pl.when(has_next)
        def _():
            start(first(d))

        if d == 1:
            masks()

    for copy in local[1:]:
        copy.wait()

    ones = {size: jnp.ones((size, HD), BF16) for size in (128, 256, 512)}

    def stage(kw, vw, bias, tiles, opening=False, between=None, unroll=8):
        def scores(head, slot):
            shared = pl.ds(pl.multiple_of(head // 8 * HD, HD), HD)
            for r, nr, k, nk, _ in tiles:
                q = qv[r : r + nr, pl.ds(pl.multiple_of(head * HD, HD), HD)]
                sb[slot, r : r + nr, 0:nk] = dot(q, kw[k : k + nk, shared], 1, 1)

        def mix(head, slot):
            shared = pl.ds(pl.multiple_of(head // 8 * HD, HD), HD)
            for r, nr, k, nk, closing in tiles:
                s = sb[slot, r : r + nr, 0:nk] * SCALE + bias[r : r + nr, k : k + nk]
                high = jnp.max(s, axis=1, keepdims=True)
                if opening:
                    new = jnp.broadcast_to(high, (nr, HD))
                else:
                    old = top[head, r : r + nr, :]
                    new = jnp.maximum(old, high)
                p = jnp.exp2(s - jnp.tile(new, (1, nk // HD))).astype(BF16)
                v = jnp.concatenate([vw[k : k + nk, shared], ones[nk]], axis=1)
                o = dot(p, v, 1, 0)
                if not opening:
                    o = acc[head, r : r + nr, :] * jnp.tile(jnp.exp2(old - new), (1, 2)) + o
                keep = nr
                if closing is not None:
                    ref, keep = closing
                    ref[:, pl.ds(pl.multiple_of(head * HD, HD), HD)] = (
                        o[keep:, 0:HD] / o[keep:, HD : 2 * HD]
                    ).astype(BF16)
                if keep:
                    acc[head, r : r + keep, :] = o[:keep]
                    top[head, r : r + keep, :] = new[:keep]

        scores(0, 0)

        def step(i, carry):
            for u in range(unroll):
                head = i * unroll + u
                scores(lax.rem(head + 1, 16), (u + 1) % 2)
                mix(head, u % 2)
            if between is not None:

                @pl.when(i == 0)
                def _():
                    between()

            return carry

        lax.fori_loop(0, 16 // unroll, step, 0)

    def forward(cond, half, pieces):
        @pl.when(cond & has_prev & (hh == half))
        def _():
            for d in pieces:
                if d > 1:
                    taken(first(d))

        @pl.when(cond & passes & (hh == half))
        def _():
            for d in pieces:
                if d // 2 != half:
                    start(second(d))

        for b in (1, 0):
            for d in pieces:
                if d // 2 == half:

                    @pl.when(cond & passes & (hh == half) & (hx[d] == b))
                    def _():
                        start(second(d, b))

    def forward_early(cond):
        forward(cond, 0, (2,))
        forward(cond, 1, (0, 1))

    def forward_late(cond):
        forward(cond, 0, (3, 1, 0))
        forward(cond, 1, (2, 3))

    def take_first(cond):
        @pl.when(has_prev & cond)
        def _():
            taken(first(0))
            taken(first(1))

    def early():
        take_first(z != 0)
        forward_early(z != 0)

    stage(ko, vo, bo, [(0, 256, 0, 256, None), (256, 256, 0, 512, None)], True, early)
    take_first(z == 0)
    forward_late(z != 0)
    stage(k1a, v1a, b1a, [(0, 512, 0, 256, None)], between=lambda: forward_early(z == 0))
    forward_late(z == 0)
    stage(k1b, v1b, b1b, [(0, 512, 0, 256, None)])

    def landed(half, d):
        @pl.when((c > 1) & (hh == half))
        def _():
            taken(second(d))

    def landed_low(b):
        for half in (0, 1):
            for d in (2 * half, 2 * half + 1):

                @pl.when((c > 1) & (hh == half) & (hx[d] == b))
                def _():
                    taken(second(d, b))

    def flushed(i, ref, r):
        return pltpu.make_async_copy(ref, out.at[r : r + ref.shape[0]], flush.at[i])

    landed(0, 2)
    landed(1, 0)
    stage(k2p, v2p, b2p, [(0, 512, 0, 128, None)])
    landed(0, 3)
    landed(1, 1)
    stage(k2q, v2q, b2q, [(0, 512, 0, 128, (ov2, 256))])
    flushed(0, ov2, 256).start()
    landed_low(1)
    stage(k21, v21, b21, [(0, 256, 0, 128, (ov1, 128))], unroll=16)
    flushed(1, ov1, 128).start()
    for d in (1, 2, 3):
        for copy in exchange(d):
            copy.wait_send()
    for d in range(4):

        @pl.when(has_next)
        def _():
            for copy in first(d):
                copy.wait_send()

    flushed(0, ov2, 256).wait()
    landed_low(0)
    stage(k20, v20, b20, [(0, 128, 0, 128, (ov0, 0))], unroll=16)
    flushed(2, ov0, 0).start()

    flushed(1, ov1, 128).wait()
    flushed(2, ov0, 0).wait()
    for d in range(4):

        @pl.when(passes)
        def _():
            for copy in second(d):
                copy.wait_send()


def place(a, b, held, came, went):
    size = a.shape[0] // PARTS

    def part(ref, i):
        return ref.at[pl.ds(i * size, size)]

    come = [pltpu.make_async_copy(part(a, i), part(held, i), came.at[i]) for i in range(PARTS)]
    go = [pltpu.make_async_copy(part(held, i), part(b, i), went.at[i]) for i in range(PARTS)]
    for copy in come:
        copy.start()
    for i in range(PARTS):
        come[i].wait()
        go[i].start()
    for copy in go:
        copy.wait()


def per_device(n, queries, keys, values, lengths):
    hbm = pl.BlockSpec(memory_space=pltpu.HBM)
    sems = pltpu.SemaphoreType.DMA((4, 2))
    attended = pl.pallas_call(
        functools.partial(kernel, n),
        out_shape=jax.ShapeDtypeStruct(queries.shape, BF16),
        in_specs=[hbm] * 4,
        out_specs=hbm,
        scratch_shapes=[pltpu.VMEM((512, 2048), BF16)]
        + [pltpu.VMEM((512, 256), BF16)] * 2
        + [pltpu.VMEM((256, 256), BF16)] * 4
        + [pltpu.VMEM((128, 256), BF16)] * 8
        + [pltpu.VMEM((512, 512), F32)]
        + [pltpu.VMEM((512, 256), F32)] * 2
        + [pltpu.VMEM((512, 128), F32)] * 2
        + [pltpu.VMEM((256, 128), F32), pltpu.VMEM((128, 128), F32)]
        + [
            pltpu.VMEM((16, 512, 256), F32),
            pltpu.VMEM((16, 512, 128), F32),
            pltpu.VMEM((2, 512, 512), F32),
            pltpu.SMEM((64,), jnp.int32),
            pltpu.SemaphoreType.DMA((4,)),
        ]
        + [sems] * 6
        + [pltpu.SemaphoreType.DMA((3,)), pltpu.VMEM((256, 2048), BF16)]
        + [pltpu.VMEM((128, 2048), BF16)] * 2,
        compiler_params=pltpu.CompilerParams(
            collective_id=0, has_side_effects=True, vmem_limit_bytes=58 * 2**20
        ),
    )(queries, keys, values, lengths)
    return pl.pallas_call(
        place,
        out_shape=jax.ShapeDtypeStruct(queries.shape, BF16),
        in_specs=[hbm],
        out_specs=hbm,
        scratch_shapes=[pltpu.VMEM(queries.shape, BF16)] + [pltpu.SemaphoreType.DMA((PARTS,))] * 2,
    )(attended)


def solution(mesh):
    placed = (P("ctx", "head"), P(("ctx", "head"), None), P(("ctx", "head"), None), P())
    return jax.shard_map(
        functools.partial(per_device, mesh.shape["ctx"]),
        mesh=mesh,
        in_specs=placed,
        out_specs=P("ctx", "head"),
        check_vma=False,
    )
```
